512 devices in a mesh: grain: 16 (over x, y_hi, core), space: 32 (over z, y_lo).
Axes of the slice: x: 4, y: 4 (y_hi: 2, y_lo: 2; y = y_hi * 2 + y_lo), z: 16, core: 2. Of those that a mesh axis runs over, the one named last changes fastest.
Arguments:
- labels: int32 [32, 256, 256], P(None, 'space'), may hold values from 0 to 63, as said below
- density: float32 [32, 256, 256], P('grain', 'space'), may hold values from 0.05 to 0.95
Outputs:
- grain_fields: float32 [64, 32, 256, 256], P('grain', None, 'space')
- density_field: float32 [32, 256, 256], P('grain', 'space')
The draws below stay inside these ranges and needn't reach their ends.
Inputs may be any that keep to these rules, and one draw needn't show every extreme that they name: Within each aligned block of 2 x 2 x 8 cells (thickness, first and second in-plane dimension) the labels take at most three values.
All inputs are finite; a program needn't handle non-finite values.
Results may differ from the reference program's by a relative error of at most 0.0001.
Values sent between devices are 32-bit elements; how exact they have to be, the bound alone decides.
No kernel may reach another device: no remote copies, remote signals or barrier semaphores. Data moves between devices by JAX's collectives and lax.ppermute only.
A program may use at most 64 MiB of HBM per device.

```python
import jax
import jax.numpy as jnp
from jax import lax

NY = 256
STEPS = 2
NSUB = 4
G = 64
Z = 32
NX = 256


def spread_blocks(coarse):
    return jnp.repeat(jnp.repeat(jnp.repeat(coarse, 2, axis=0), 2, axis=1), 8, axis=2)


def draw_labels(key, part):
    key = jax.random.fold_in(key, 11)
    first_key, second_key, third_key, flip_key = jax.random.split(key, 4)
    coarse_shape = (Z // 2, NX // 2, NY // 8)
    first = jax.random.randint(first_key, coarse_shape, 0, G, dtype=jnp.int32)
    second = (first + jax.random.randint(second_key, coarse_shape, 1, G, dtype=jnp.int32)) % G
    third = (first + jax.random.randint(third_key, coarse_shape, 1, G, dtype=jnp.int32)) % G
    first = spread_blocks(first)
    second = spread_blocks(second)
    third = spread_blocks(third)
    zpos = jnp.arange(Z, dtype=jnp.int32)[:, None, None]
    xpos = jnp.arange(NX, dtype=jnp.int32)[None, :, None]
    ypos = jnp.arange(NY, dtype=jnp.int32)[None, None, :]
    parity = (zpos + xpos + ypos) % 2
    flipped = jax.random.randint(flip_key, (Z, NX, NY), 0, 8, dtype=jnp.int32) == 0
    checker = jnp.where(parity == 0, first, second)
    return jnp.where(flipped, third, checker).astype(jnp.int32)


def draw_density(key, part):
    key = jax.random.fold_in(key, 23)
    mode_key, value_key = jax.random.split(key)
    upper = jax.random.randint(mode_key, (Z, NX, NY), 0, 2, dtype=jnp.int32)
    unit = jax.random.uniform(value_key, (Z, NX, NY), jnp.float32)
    spread = 0.2
    lower_value = 0.05 + spread * unit
    upper_value = 0.95 - spread * unit
    return jnp.where(upper == 1, upper_value, lower_value).astype(jnp.float32)


def setup_inputs(seed: int = 0) -> dict:
    key_of = jax.random.split(jax.random.key(seed), 3)
    labels = draw_labels(jax.random.fold_in(key_of[2], 71), 0)
    density = draw_density(jax.random.fold_in(key_of[2], 71), 0)
    return {"labels": labels, "density": density}


bulk_coef = 8.0
grain_coef = 1.0
grad_density = 1.0
grad_grain = 1.0
mobility = 1.0
relax_rate = 2.0
grain_step = 0.008
density_step = 0.004


def roll_laplace(field):
    total = jnp.zeros_like(field)
    for axis in range(3):
        total = total + (jnp.roll(field, 1, axis) + jnp.roll(field, -1, axis))
    return total - 6.0 * field


def grain_rate(order, dens, square):
    return grain_coef * (12.0 * (1.0 - dens) * order - 12.0 * (2.0 - dens) * order * order + 12.0 * order * square)


def bulk_potential(dens, square, cube):
    return bulk_coef * (2.0 * dens * (1.0 - dens) * (1.0 - dens) - 2.0 * dens * dens * (1.0 - dens)) + grain_coef * (2.0 * dens - 6.0 * square + 4.0 * cube)


def reference(labels, density):
    grain_ids = jnp.arange(G, dtype=jnp.int32)
    dens = density
    orders = jnp.where(labels[None] == grain_ids[:, None, None, None], dens[None], jnp.zeros_like(dens)[None])
    square = jnp.sum(orders * orders, axis=0)
    for step in range(STEPS):
        def relax(order):
            return order - grain_step * relax_rate * (grain_rate(order, dens, square) - grad_grain * roll_laplace(order))
        orders = lax.map(relax, orders)
        square = jnp.sum(orders * orders, axis=0)
        cube = jnp.sum(orders * orders * orders, axis=0)
        for sub in range(NSUB):
            potential = bulk_potential(dens, square, cube) - grad_density * roll_laplace(dens)
            dens = dens + density_step * mobility * roll_laplace(potential)
    return orders, dens
```

```python
import functools

import jax
import jax.numpy as jnp
from jax import lax
from jax.experimental import pallas as pl
from jax.experimental.pallas import tpu as pltpu
from jax.sharding import PartitionSpec as P

GDEV = 4
NSUB = 4
LAYERS = 32
WIDTH = 256
ROWS = 56
MID = 24
TILE = 15
BASE = 6

rate = 0.008 * 2.0
density_step = 0.004

SHIFTS = (
    (0, 0),
    (1, 0),
    (-1, 0),
    (0, 1),
    (0, -1),
    (1, 1),
    (1, -1),
    (-1, 1),
    (-1, -1),
    (2, 0),
    (-2, 0),
    (0, 2),
    (0, -2),
)
SLOT = {pair: index for index, pair in enumerate(SHIFTS)}
INNER = ((0, 0, 0), (1, 0, 0), (-1, 0, 0), (0, 1, 0), (0, -1, 0), (0, 0, 1), (0, 0, -1))
OUTER = tuple(
    (dz, dx, dy)
    for dz in range(-2, 3)
    for dx in range(-2, 3)
    for dy in range(-2, 3)
    if abs(dz) + abs(dx) + abs(dy) == 2
)


def rolled(x, offset, axis):
    size = x.shape[axis]
    return pltpu.roll(x, (-offset) % size, axis)


def centre_weight(c):
    return c * ((1.0 / rate - 18.0) + c * (36.0 - 24.0 * c))


def wrap(layer):
    return lax.bitwise_and(layer, LAYERS - 1)


def stencil(ref, layer, row, count):
    here = ref[layer, row : row + count, :]
    return here, (
        ref[wrap(layer + 1), row : row + count, :],
        ref[wrap(layer - 1), row : row + count, :],
        ref[layer, row + 1 : row + 1 + count, :],
        ref[layer, row - 1 : row - 1 + count, :],
        rolled(here, 1, 1),
        rolled(here, -1, 1),
    )


def six(parts):
    return (parts[0] + parts[1]) + (parts[2] + parts[3]) + (parts[4] + parts[5])


def class_sums(labels, weights):
    square = None
    cube = None
    count = len(labels)
    for i in range(count):
        total = weights[i]
        for j in range(i + 1, count):
            total = total + jnp.where(labels[i] == labels[j], weights[j], 0.0)
        rest = total - weights[i]
        both = total + rest
        part2 = weights[i] * both
        part3 = weights[i] * (both * both - total * rest)
        square = part2 if square is None else square + part2
        cube = part3 if cube is None else cube + part3
    return square, cube


def first_sums(lab_ref, c_ref, layer, row, count):
    c, cs = stencil(c_ref, layer, row, count)
    lab, labs = stencil(lab_ref, layer, row, count)
    return (lab,) + labs, (centre_weight(c),) + cs


def kernel(
    where_ref,
    labels_ref,
    dens_ref,
    near_ref,
    far_ref,
    grains_ref,
    out_ref,
    lab,
    c0,
    c1,
    mu,
    k1,
    s2,
    k2,
    lab_copies,
    c_copies,
    w_copies,
    eta_mid,
    eta_edge,
):
    grain = where_ref[0]
    core = lax.rem(grain, 2)
    start = 2 * grain - TILE + LAYERS

    def place(layer, carry):
        z = wrap(start + layer)
        lab[layer, MID : MID + 8, :] = labels_ref[z].astype(jnp.float32)
        c0[layer, MID : MID + 8, :] = dens_ref[z]
        up = 1 - core
        for which, ref in ((0, lab), (1, c0)):
            for block in (0, 1):
                mine = near_ref[which, block, z]
                other = far_ref[which, block, z]
                plus = jnp.where(core == 0, mine, other)
                minus = jnp.where(core == 0, other, mine)
                ref[layer, MID + 8 * (block + 1) : MID + 8 * (block + 2), :] = plus
                ref[layer, MID - 8 * (block + 1) : MID - 8 * block, :] = minus
        return carry

    lax.fori_loop(0, LAYERS, place, 0)

    grain_ids = [(grain * GDEV + g).astype(jnp.float32) for g in range(GDEV)]

    def own_grains(labels, weights):
        result = []
        for g in range(GDEV):
            total = None
            for one, weight in zip(labels, weights):
                part = jnp.where(one == grain_ids[g], weight, 0.0)
                total = part if total is None else total + part
            result.append(rate * total)
        return result

    def store_sums(layer, row, square, cube):
        square = (rate * rate) * square
        k1[layer, row : row + 8, :] = (4.0 * rate**3) * cube - 6.0 * square
        return square

    def sums_all(layer, carry):
        for row in (MID - 8, MID, MID + 8):
            labels, weights = first_sums(lab, c0, layer, row, 8)
            square = store_sums(layer, row, *class_sums(labels, weights))
            s2[layer, row : row + 8, :] = square
            if row == MID:
                for g, value in enumerate(own_grains(labels, weights)):
                    eta_mid[g, layer] = value
        return carry

    lax.fori_loop(0, LAYERS, sums_all, 0)

    def sums_far(layer, carry):
        for row in (MID - 16, MID + 16):
            labels, weights = first_sums(lab, c0, layer, row, 8)
            store_sums(layer, row, *class_sums(labels, weights))
        return carry

    lax.fori_loop(TILE - 6, TILE + 8, sums_far, 0)

    sub = lax.broadcasted_iota(jnp.int32, (8, WIDTH), 0)
    upper = sub < 4

    def edge_grains(layer, carry):
        low_labels, low_weights = first_sums(lab, c0, layer, MID - 8, 8)
        high_labels, high_weights = first_sums(lab, c0, layer, MID + 8, 8)
        labels = [jnp.where(upper, h, w) for h, w in zip(high_labels, low_labels)]
        weights = [jnp.where(upper, h, w) for h, w in zip(high_weights, low_weights)]
        for g, value in enumerate(own_grains(labels, weights)):
            eta_edge[g, layer] = value
        return carry

    lax.fori_loop(0, LAYERS, edge_grains, 0)

    def mu_at(source, extra, layer, row):
        c, cs = stencil(source, layer, row, 8)
        bulk = c * (24.0 + c * (32.0 * c - 48.0)) + extra[layer, row : row + 8, :]
        mu[layer, row : row + 8, :] = bulk - six(cs)

    def c_at(source, layer, row):
        m, ms = stencil(mu, layer, row, 8)
        c = source[layer, row : row + 8, :]
        return c + density_step * (six(ms) - 6.0 * m)

    def over(low, high, rows, body):
        if high > low and rows:

            def step(layer, carry):
                for row in rows:
                    body(layer, row)
                return carry

            lax.fori_loop(low, high, step, 0)

    sides = (MID - 8, MID + 8)
    fars = (MID - 16, MID + 16)

    def near_tile(distance):
        return TILE - distance, TILE + 2 + distance

    for sub_step in range(1, NSUB + 1):
        source = c0 if sub_step == 1 else c1

        def put_mu(layer, row, source=source):
            mu_at(source, k1, layer, row)

        def put_c(layer, row, source=source):
            c1[layer, row : row + 8, :] = c_at(source, layer, row)

        over(0, LAYERS, (MID,) + sides, put_mu)
        if 8 - 2 * sub_step >= 0:
            over(*near_tile(8 - 2 * sub_step), fars, put_mu)
        if sub_step < NSUB:
            over(0, LAYERS, (MID,) + sides, put_c)
            if 7 - 2 * sub_step >= 0:
                over(*near_tile(7 - 2 * sub_step), fars, put_c)
        else:
            over(0, LAYERS, (MID,), put_c)
            over(*near_tile(7), sides, put_c)

    def grain_steps(layer, carry):
        c = c1[layer, MID : MID + 8, :]
        square = s2[layer, MID : MID + 8, :]
        linear = 1.0 - rate * (12.0 * (1.0 - c) + 12.0 * square + 6.0)
        quadratic = (12.0 * rate) * (2.0 - c)
        for g in range(GDEV):
            mid = eta_mid[g, layer]
            edge = eta_edge[g, layer]
            after = jnp.where(sub == 7, rolled(edge, 1, 0), rolled(mid, 1, 0))
            before = jnp.where(sub == 0, rolled(edge, -1, 0), rolled(mid, -1, 0))
            around = six(
                (
                    eta_mid[g, wrap(layer + 1)],
                    eta_mid[g, wrap(layer - 1)],
                    after,
                    before,
                    rolled(mid, 1, 1),
                    rolled(mid, -1, 1),
                )
            )
            grains_ref[g, wrap(start + layer)] = (
                mid * (linear + quadratic * mid) + rate * around
            )
        return carry

    lax.fori_loop(0, LAYERS, grain_steps, 0)

    def copies(index, carry):
        layer = index + BASE
        c_wide = c0[layer, MID - 16 : MID + 24, :]
        lab_wide = lab[layer, MID - 16 : MID + 24, :]
        c_cols = {dy: c_wide if dy == 0 else rolled(c_wide, dy, 1) for dy in range(-2, 3)}
        lab_cols = {dy: lab_wide if dy == 0 else rolled(lab_wide, dy, 1) for dy in range(-2, 3)}
        for slot, (dx, dy) in enumerate(SHIFTS):
            c = c_cols[dy] if dx == 0 else rolled(c_cols[dy], dx, 0)
            one = lab_cols[dy] if dx == 0 else rolled(lab_cols[dy], dx, 0)
            c = c[8:32]
            lab_copies[slot, index] = one[8:32]
            if abs(dx) + abs(dy) < 2:
                w_copies[slot, index] = centre_weight(c)
            c_copies[slot, index] = 2.0 * c if abs(dx) + abs(dy) == 2 and dx * dy else c
        return carry

    lax.fori_loop(0, 20, copies, 0)

    def second_sums(load, c, square):
        labels = [load(lab_copies, cell) for cell in INNER + OUTER]
        first = [load(w_copies, INNER[0])] + [load(c_copies, cell) for cell in INNER[1:]]
        spread = [6.0 * load(c_copies, INNER[0])] + [load(w_copies, cell) for cell in INNER[1:]]
        for cell in OUTER:
            value = load(c_copies, cell)
            if cell[0] in (1, -1):
                value = value + value
            spread.append(value)
        linear = rate - (rate * rate) * (12.0 * (1.0 - c) + 12.0 * square + 6.0)
        quadratic = (12.0 * rate**3) * (2.0 - c)
        inner = None
        outer = None
        for i in range(25):
            total = spread[i]
            own = first[i] if i < 7 else None
            for j in range(i + 1, 25):
                same = labels[i] == labels[j]
                total = total + jnp.where(same, spread[j], 0.0)
                if j < 7:
                    own = own + jnp.where(same, first[j], 0.0)
            rest = total - spread[i]
            if i < 7:
                own_rest = own - first[i]
                value = own * (linear + quadratic * own) + (rate * rate) * total
                value_rest = own_rest * (linear + quadratic * own_rest) + (rate * rate) * rest
                part = value * value * (4.0 * value - 6.0) - value_rest * value_rest * (
                    4.0 * value_rest - 6.0
                )
                inner = part if inner is None else inner + part
            else:
                both = total + rest
                part = spread[i] * (
                    both * ((4.0 * rate * rate) * both - 6.0)
                    - (4.0 * rate * rate) * (total * rest)
                )
                outer = part if outer is None else outer + part
        return inner + (rate**4) * outer

    def load_block(layer, block, lanes):
        def load(ref, cell):
            dz, dx, dy = cell
            return ref[SLOT[dx, dy], layer - BASE + dz, 8 * block : 8 * block + 8, lanes]

        return load

    def halves(low, high, body):
        def step(index, carry):
            lanes = pl.ds(pl.multiple_of(128 * lax.rem(index, 2), 128), 128)
            body(lax.div(index, 2), lanes)
            return carry

        lax.fori_loop(2 * low, 2 * high, step, 0)

    def plain(block):
        row = MID - 8 + 8 * block

        def body(layer, lanes):
            k2[layer, row : row + 8, lanes] = second_sums(
                load_block(layer, block, lanes),
                c1[layer, row : row + 8, lanes],
                s2[layer, row : row + 8, lanes],
            )

        return body

    def merged(layer, lanes):
        high = load_block(layer, 2, lanes)
        low = load_block(layer, 0, lanes)
        pick = lax.broadcasted_iota(jnp.int32, (8, 128), 0) < 4

        def load(ref, cell):
            return jnp.where(pick, high(ref, cell), low(ref, cell))

        value = second_sums(
            load,
            jnp.where(pick, c1[layer, MID + 8 : MID + 16, lanes], c1[layer, MID - 8 : MID, lanes]),
            jnp.where(pick, s2[layer, MID + 8 : MID + 16, lanes], s2[layer, MID - 8 : MID, lanes]),
        )
        k2[layer, MID + 8 : MID + 16, lanes] = value
        k2[layer, MID - 8 : MID, lanes] = value

    halves(TILE - 7, TILE + 9, plain(1))
    halves(TILE - 2, TILE + 4, plain(0))
    halves(TILE - 2, TILE + 4, plain(2))
    halves(TILE - 6, TILE - 2, merged)
    halves(TILE + 4, TILE + 8, merged)

    for sub_step in range(1, NSUB + 1):

        def put_mu(layer, row):
            mu_at(c1, k2, layer, row)

        def put_c(layer, row):
            c1[layer, row : row + 8, :] = c_at(c1, layer, row)

        over(*near_tile(9 - 2 * sub_step), (MID,), put_mu)
        over(*near_tile(8 - 2 * sub_step), sides, put_mu)
        if sub_step < NSUB:
            over(*near_tile(8 - 2 * sub_step), (MID,), put_c)
            over(*near_tile(7 - 2 * sub_step), sides, put_c)
        else:
            for layer in (0, 1):
                out_ref[layer] = c_at(c1, TILE + layer, MID)


def sintering(where, labels, dens, near, far):
    field = pltpu.VMEM((LAYERS, ROWS, WIDTH), jnp.float32)
    vmem = pl.BlockSpec(memory_space=pltpu.VMEM)
    return pl.pallas_call(
        kernel,
        out_shape=(
            jax.ShapeDtypeStruct((GDEV, LAYERS, 8, WIDTH), jnp.float32),
            jax.ShapeDtypeStruct((2, 8, WIDTH), jnp.float32),
        ),
        in_specs=[pl.BlockSpec(memory_space=pltpu.SMEM)] + [vmem] * 4,
        out_specs=(vmem, vmem),
        scratch_shapes=[field] * 7
        + [
            pltpu.VMEM((13, 20, 24, WIDTH), jnp.float32),
            pltpu.VMEM((13, 20, 24, WIDTH), jnp.float32),
            pltpu.VMEM((5, 20, 24, WIDTH), jnp.float32),
            pltpu.VMEM((GDEV, LAYERS, 8, WIDTH), jnp.float32),
            pltpu.VMEM((GDEV, LAYERS, 8, WIDTH), jnp.float32),
        ],
        compiler_params=pltpu.CompilerParams(vmem_limit_bytes=56 * 1024 * 1024),
        name="sintering",
    )(where, labels, dens, near, far)


def from_sides(block, distance):
    grains = lax.axis_size("grain")
    count = lax.axis_size("space")
    pairs = []
    for g in range(grains):
        way = distance if g % 2 == 0 else -distance
        for s in range(count):
            pairs.append((g * count + (s + way) % count, g * count + s))
    return lax.ppermute(block, ("grain", "space"), pairs)


def swap_cores(block):
    return lax.ppermute(block, "grain", [(i, i ^ 1) for i in range(lax.axis_size("grain"))])


def per_device(labels, density):
    grain = lax.axis_index("grain")
    named = labels.astype(jnp.float32)
    own = jnp.broadcast_to(density[None], (lax.axis_size("grain"),) + density.shape)
    dens = lax.all_to_all(own, "grain", 0, 0).reshape(LAYERS, 8, WIDTH)
    named_sides = [from_sides(named, distance) for distance in (1, 2)]
    dens_sides = [from_sides(dens, distance) for distance in (1, 2)]
    near = jnp.stack([jnp.stack(named_sides), jnp.stack(dens_sides)])
    far = swap_cores(near)
    return sintering(grain.reshape(1).astype(jnp.int32), labels, dens, near, far)


def solution(mesh):
    return jax.shard_map(
        per_device,
        mesh=mesh,
        in_specs=(P(None, "space", None), P("grain", "space", None)),
        out_specs=(P("grain", None, "space", None), P("grain", "space", None)),
        check_vma=False,
    )
```

```python
import functools

import jax
import jax.numpy as jnp
from jax import lax
from jax.experimental import pallas as pl
from jax.experimental.pallas import tpu as pltpu
from jax.sharding import PartitionSpec as P

GDEV = 4
NSUB = 4
LAYERS = 32
DEEP = 34
WIDTH = 256
ROWS = 56
MID = 24
TILE = 16
BASE = 7
GROUP = 4

rate = 0.008 * 2.0
density_step = 0.004

SHIFTS = (
    (0, 0),
    (1, 0),
    (-1, 0),
    (0, 1),
    (0, -1),
    (1, 1),
    (1, -1),
    (-1, 1),
    (-1, -1),
    (2, 0),
    (-2, 0),
    (0, 2),
    (0, -2),
)
SLOT = {pair: index for index, pair in enumerate(SHIFTS)}
INNER = ((0, 0, 0), (1, 0, 0), (-1, 0, 0), (0, 1, 0), (0, -1, 0), (0, 0, 1), (0, 0, -1))
OUTER = tuple(
    (dz, dx, dy)
    for dz in range(-2, 3)
    for dx in range(-2, 3)
    for dy in range(-2, 3)
    if abs(dz) + abs(dx) + abs(dy) == 2
)


def rolled(x, offset, axis):
    size = x.shape[axis]
    return pltpu.roll(x, (-offset) % size, axis)


def centre_weight(c):
    return c * ((1.0 / rate - 18.0) + c * (36.0 - 24.0 * c))


def wrap(layer):
    return lax.bitwise_and(layer, LAYERS - 1)


def stencil(ref, layer, row, count):
    here = ref[layer, row : row + count, :]
    return here, (
        ref[layer + 1, row : row + count, :],
        ref[layer - 1, row : row + count, :],
        ref[layer, row + 1 : row + 1 + count, :],
        ref[layer, row - 1 : row - 1 + count, :],
        rolled(here, 1, 1),
        rolled(here, -1, 1),
    )


def six(parts):
    return (parts[0] + parts[1]) + (parts[2] + parts[3]) + (parts[4] + parts[5])


def class_sums(labels, weights):
    square = None
    cube = None
    count = len(labels)
    for i in range(count):
        total = weights[i]
        for j in range(i + 1, count):
            total = total + jnp.where(labels[i] == labels[j], weights[j], 0.0)
        rest = total - weights[i]
        both = total + rest
        part2 = weights[i] * both
        part3 = weights[i] * (both * both - total * rest)
        square = part2 if square is None else square + part2
        cube = part3 if cube is None else cube + part3
    return square, cube


def first_sums(lab_ref, c_ref, layer, row, count):
    c, cs = stencil(c_ref, layer, row, count)
    lab, labs = stencil(lab_ref, layer, row, count)
    return (lab,) + labs, (centre_weight(c),) + cs


def chunks(low, high, body, group):
    count = high - low
    while count % group:
        group -= 1

    def step(index, carry):
        for k in range(group):
            body(low + index * group + k)
        return carry

    lax.fori_loop(0, count // group, step, 0)


def close_ends(ref, rows):
    ref[0, rows, :] = ref[LAYERS, rows, :]
    ref[LAYERS + 1, rows, :] = ref[1, rows, :]


def kernel(
    where_ref,
    labels_ref,
    dens_ref,
    near_ref,
    far_ref,
    grains_ref,
    out_ref,
    lab,
    c0,
    c1,
    cx,
    mu,
    k1,
    s2,
    k2,
    lab_copies,
    c_copies,
    w_copies,
    eta_mid,
    eta_edge,
):
    grain = where_ref[0]
    core = lax.rem(grain, 2)
    start = 2 * grain - TILE + LAYERS

    def place(layer):
        z = wrap(start + layer)
        lab[layer, MID : MID + 8, :] = labels_ref[z].astype(jnp.float32)
        c0[layer, MID : MID + 8, :] = dens_ref[z]
        up = 1 - core
        for which, ref in ((0, lab), (1, c0)):
            for block in (0, 1):
                mine = near_ref[which, block, z]
                other = far_ref[which, block, z]
                plus = jnp.where(core == 0, mine, other)
                minus = jnp.where(core == 0, other, mine)
                ref[layer, MID + 8 * (block + 1) : MID + 8 * (block + 2), :] = plus
                ref[layer, MID - 8 * (block + 1) : MID - 8 * block, :] = minus

    chunks(0, DEEP, place, 2)

    grain_ids = [(grain * GDEV + g).astype(jnp.float32) for g in range(GDEV)]

    def own_grains(labels, weights):
        result = []
        for g in range(GDEV):
            total = None
            for one, weight in zip(labels, weights):
                part = jnp.where(one == grain_ids[g], weight, 0.0)
                total = part if total is None else total + part
            result.append(rate * total)
        return result

    def store_sums(layer, row, square, cube):
        square = (rate * rate) * square
        k1[layer, row : row + 8, :] = (4.0 * rate**3) * cube - 6.0 * square
        return square

    def sums_all(layer):
        for row in (MID - 8, MID, MID + 8):
            labels, weights = first_sums(lab, c0, layer, row, 8)
            square = store_sums(layer, row, *class_sums(labels, weights))
            s2[layer, row : row + 8, :] = square
            if row == MID:
                for g, value in enumerate(own_grains(labels, weights)):
                    eta_mid[g, layer] = value

    chunks(1, LAYERS + 1, sums_all, 1)
    for g in range(GDEV):
        eta_mid[g, 0] = eta_mid[g, LAYERS]
        eta_mid[g, LAYERS + 1] = eta_mid[g, 1]

    def sums_far(layer):
        for row in (MID - 16, MID + 16):
            labels, weights = first_sums(lab, c0, layer, row, 8)
            store_sums(layer, row, *class_sums(labels, weights))

    chunks(TILE - 6, TILE + 8, sums_far, 1)

    sub = lax.broadcasted_iota(jnp.int32, (8, WIDTH), 0)
    upper = sub < 4

    def edge_stencil(ref, layer):
        def both(z, offset):
            return jnp.where(
                upper,
                ref[z, MID + 8 + offset : MID + 16 + offset, :],
                ref[z, MID - 8 + offset : MID + offset, :],
            )

        here = both(layer, 0)
        return here, (
            both(layer + 1, 0),
            both(layer - 1, 0),
            both(layer, 1),
            both(layer, -1),
            rolled(here, 1, 1),
            rolled(here, -1, 1),
        )

    def edge_grains(layer):
        c, cs = edge_stencil(c0, layer)
        one, ones = edge_stencil(lab, layer)
        for g, value in enumerate(own_grains((one,) + ones, (centre_weight(c),) + cs)):
            eta_edge[g, layer] = value

    chunks(1, LAYERS + 1, edge_grains, 2)

    def mu_at(source, extra, layer, row):
        c, cs = stencil(source, layer, row, 8)
        bulk = c * (24.0 + c * (32.0 * c - 48.0)) + extra[layer, row : row + 8, :]
        mu[layer, row : row + 8, :] = bulk - six(cs)

    def c_at(source, layer, row):
        m, ms = stencil(mu, layer, row, 8)
        c = source[layer, row : row + 8, :]
        return c + density_step * (six(ms) - 6.0 * m)

    def over(low, high, rows, body):
        if high > low and rows:

            def step(layer):
                for row in rows:
                    body(layer, row)

            chunks(low, high, step, GROUP if len(rows) > 1 else 2 * GROUP)

    sides = (MID - 8, MID + 8)
    fars = (MID - 16, MID + 16)

    def near_tile(distance):
        return TILE - distance, TILE + 2 + distance

    near_rows = slice(MID - 8, MID + 16)
    for sub_step in range(1, NSUB + 1):
        source = c0 if sub_step == 1 else (cx, c1)[sub_step % 2]
        target = (c1, cx)[sub_step % 2]

        def put_mu(layer, row, source=source):
            mu_at(source, k1, layer, row)

        def put_c(layer, row, source=source, target=target):
            target[layer, row : row + 8, :] = c_at(source, layer, row)

        over(1, LAYERS + 1, (MID,) + sides, put_mu)
        close_ends(mu, near_rows)
        if 8 - 2 * sub_step >= 0:
            over(*near_tile(8 - 2 * sub_step), fars, put_mu)
        if sub_step < NSUB:
            over(1, LAYERS + 1, (MID,) + sides, put_c)
            close_ends(target, near_rows)
            if 7 - 2 * sub_step >= 0:
                over(*near_tile(7 - 2 * sub_step), fars, put_c)
        else:
            over(1, LAYERS + 1, (MID,), put_c)
            over(*near_tile(7), sides, put_c)

    def grain_steps(layer):
        c = c1[layer, MID : MID + 8, :]
        square = s2[layer, MID : MID + 8, :]
        linear = 1.0 - rate * (12.0 * (1.0 - c) + 12.0 * square + 6.0)
        quadratic = (12.0 * rate) * (2.0 - c)
        for g in range(GDEV):
            mid = eta_mid[g, layer]
            edge = eta_edge[g, layer]
            after = jnp.where(sub == 7, rolled(edge, 1, 0), rolled(mid, 1, 0))
            before = jnp.where(sub == 0, rolled(edge, -1, 0), rolled(mid, -1, 0))
            around = six(
                (
                    eta_mid[g, layer + 1],
                    eta_mid[g, layer - 1],
                    after,
                    before,
                    rolled(mid, 1, 1),
                    rolled(mid, -1, 1),
                )
            )
            grains_ref[g, wrap(start + layer)] = (
                mid * (linear + quadratic * mid) + rate * around
            )

    chunks(1, LAYERS + 1, grain_steps, 2)

    def copies(index):
        layer = index + BASE
        c_wide = c0[layer, MID - 16 : MID + 24, :]
        lab_wide = lab[layer, MID - 16 : MID + 24, :]
        c_cols = {dy: c_wide if dy == 0 else rolled(c_wide, dy, 1) for dy in range(-2, 3)}
        lab_cols = {dy: lab_wide if dy == 0 else rolled(lab_wide, dy, 1) for dy in range(-2, 3)}
        for slot, (dx, dy) in enumerate(SHIFTS):
            c = c_cols[dy] if dx == 0 else rolled(c_cols[dy], dx, 0)
            one = lab_cols[dy] if dx == 0 else rolled(lab_cols[dy], dx, 0)
            c = c[8:32]
            lab_copies[slot, index] = one[8:32]
            if abs(dx) + abs(dy) < 2:
                w_copies[slot, index] = centre_weight(c)
            c_copies[slot, index] = 2.0 * c if abs(dx) + abs(dy) == 2 and dx * dy else c

    chunks(0, 20, copies, 1)

    def second_sums(load, c, square):
        labels = [load(lab_copies, cell) for cell in INNER + OUTER]
        first = [load(w_copies, INNER[0])] + [load(c_copies, cell) for cell in INNER[1:]]
        spread = [6.0 * load(c_copies, INNER[0])] + [load(w_copies, cell) for cell in INNER[1:]]
        for cell in OUTER:
            value = load(c_copies, cell)
            if cell[0] in (1, -1):
                value = value + value
            spread.append(value)
        linear = rate - (rate * rate) * (12.0 * (1.0 - c) + 12.0 * square + 6.0)
        quadratic = (12.0 * rate**3) * (2.0 - c)
        inner = None
        outer = None
        for i in range(25):
            total = spread[i]
            own = first[i] if i < 7 else None
            for j in range(i + 1, 25):
                same = labels[i] == labels[j]
                total = total + jnp.where(same, spread[j], 0.0)
                if j < 7:
                    own = own + jnp.where(same, first[j], 0.0)
            rest = total - spread[i]
            if i < 7:
                own_rest = own - first[i]
                value = own * (linear + quadratic * own) + (rate * rate) * total
                value_rest = own_rest * (linear + quadratic * own_rest) + (rate * rate) * rest
                part = value * value * (4.0 * value - 6.0) - value_rest * value_rest * (
                    4.0 * value_rest - 6.0
                )
                inner = part if inner is None else inner + part
            else:
                both = total + rest
                part = spread[i] * (
                    both * ((4.0 * rate * rate) * both - 6.0)
                    - (4.0 * rate * rate) * (total * rest)
                )
                outer = part if outer is None else outer + part
        return inner + (rate**4) * outer

    def load_block(layer, block, lanes):
        def load(ref, cell):
            dz, dx, dy = cell
            return ref[SLOT[dx, dy], layer - BASE + dz, 8 * block : 8 * block + 8, lanes]

        return load

    def halves(low, high, body):
        def step(index, carry):
            lanes = pl.ds(pl.multiple_of(128 * lax.rem(index, 2), 128), 128)
            body(lax.div(index, 2), lanes)
            return carry

        lax.fori_loop(2 * low, 2 * high, step, 0)

    def plain(block):
        row = MID - 8 + 8 * block

        def body(layer, lanes):
            k2[layer, row : row + 8, lanes] = second_sums(
                load_block(layer, block, lanes),
                c1[layer, row : row + 8, lanes],
                s2[layer, row : row + 8, lanes],
            )

        return body

    def merged(layer, lanes):
        high = load_block(layer, 2, lanes)
        low = load_block(layer, 0, lanes)
        pick = lax.broadcasted_iota(jnp.int32, (8, 128), 0) < 4

        def load(ref, cell):
            return jnp.where(pick, high(ref, cell), low(ref, cell))

        value = second_sums(
            load,
            jnp.where(pick, c1[layer, MID + 8 : MID + 16, lanes], c1[layer, MID - 8 : MID, lanes]),
            jnp.where(pick, s2[layer, MID + 8 : MID + 16, lanes], s2[layer, MID - 8 : MID, lanes]),
        )
        k2[layer, MID + 8 : MID + 16, lanes] = value
        k2[layer, MID - 8 : MID, lanes] = value

    halves(TILE - 7, TILE + 9, plain(1))
    halves(TILE - 2, TILE + 4, plain(0))
    halves(TILE - 2, TILE + 4, plain(2))
    halves(TILE - 6, TILE - 2, merged)
    halves(TILE + 4, TILE + 8, merged)

    for sub_step in range(1, NSUB + 1):
        source = (cx, c1)[sub_step % 2]
        target = (c1, cx)[sub_step % 2]

        def put_mu(layer, row, source=source):
            mu_at(source, k2, layer, row)

        def put_c(layer, row, source=source, target=target):
            target[layer, row : row + 8, :] = c_at(source, layer, row)

        over(*near_tile(9 - 2 * sub_step), (MID,), put_mu)
        over(*near_tile(8 - 2 * sub_step), sides, put_mu)
        if sub_step < NSUB:
            over(*near_tile(8 - 2 * sub_step), (MID,), put_c)
            over(*near_tile(7 - 2 * sub_step), sides, put_c)
        else:
            for layer in (0, 1):
                out_ref[layer] = c_at(source, TILE + layer, MID)


def sintering(where, labels, dens, near, far):
    field = pltpu.VMEM((DEEP, ROWS, WIDTH), jnp.float32)
    vmem = pl.BlockSpec(memory_space=pltpu.VMEM)
    return pl.pallas_call(
        kernel,
        out_shape=(
            jax.ShapeDtypeStruct((GDEV, LAYERS, 8, WIDTH), jnp.float32),
            jax.ShapeDtypeStruct((2, 8, WIDTH), jnp.float32),
        ),
        in_specs=[pl.BlockSpec(memory_space=pltpu.SMEM)] + [vmem] * 4,
        out_specs=(vmem, vmem),
        scratch_shapes=[field] * 8
        + [
            pltpu.VMEM((13, 20, 24, WIDTH), jnp.float32),
            pltpu.VMEM((13, 20, 24, WIDTH), jnp.float32),
            pltpu.VMEM((5, 20, 24, WIDTH), jnp.float32),
            pltpu.VMEM((GDEV, DEEP, 8, WIDTH), jnp.float32),
            pltpu.VMEM((GDEV, DEEP, 8, WIDTH), jnp.float32),
        ],
        compiler_params=pltpu.CompilerParams(vmem_limit_bytes=56 * 1024 * 1024),
        name="sintering",
    )(where, labels, dens, near, far)


def from_sides(block, distance):
    grains = lax.axis_size("grain")
    count = lax.axis_size("space")
    pairs = []
    for g in range(grains):
        way = distance if g % 2 == 0 else -distance
        for s in range(count):
            pairs.append((g * count + (s + way) % count, g * count + s))
    return lax.ppermute(block, ("grain", "space"), pairs)


def swap_cores(block):
    return lax.ppermute(block, "grain", [(i, i ^ 1) for i in range(lax.axis_size("grain"))])


def per_device(labels, density):
    grain = lax.axis_index("grain")
    named = labels.astype(jnp.float32)
    own = jnp.broadcast_to(density[None], (lax.axis_size("grain"),) + density.shape)
    dens = lax.all_to_all(own, "grain", 0, 0).reshape(LAYERS, 8, WIDTH)
    named_sides = [from_sides(named, distance) for distance in (1, 2)]
    dens_sides = [from_sides(dens, distance) for distance in (1, 2)]
    near = jnp.stack([jnp.stack(named_sides), jnp.stack(dens_sides)])
    far = swap_cores(near)
    return sintering(grain.reshape(1).astype(jnp.int32), labels, dens, near, far)


def solution(mesh):
    return jax.shard_map(
        per_device,
        mesh=mesh,
        in_specs=(P(None, "space", None), P("grain", "space", None)),
        out_specs=(P("grain", None, "space", None), P("grain", "space", None)),
        check_vma=False,
    )
```

```python
import functools

import jax
import jax.numpy as jnp
from jax import lax
from jax.experimental import pallas as pl
from jax.experimental.pallas import tpu as pltpu
from jax.sharding import PartitionSpec as P

GDEV = 4
NSUB = 4
LAYERS = 32
DEEP = 34
WIDTH = 256
HALF = 128
ROWS = 56
MID = 24
TILE = 16
BASE = 7
GROUP = 32

rate = 0.008 * 2.0
density_step = 0.004

INNER = ((0, 0, 0), (1, 0, 0), (-1, 0, 0), (0, 1, 0), (0, -1, 0), (0, 0, 1), (0, 0, -1))
OUTER = tuple(
    (dz, dx, dy)
    for dz in range(-2, 3)
    for dx in range(-2, 3)
    for dy in range(-2, 3)
    if abs(dz) + abs(dx) + abs(dy) == 2
)


def rolled(x, offset, axis):
    size = x.shape[axis]
    return pltpu.roll(x, (-offset) % size, axis)


def along(pair, offset):
    left, right = rolled(pair[0], offset, 1), rolled(pair[1], offset, 1)
    lane = lax.broadcasted_iota(jnp.int32, left.shape, 1)
    if offset > 0:
        same = lane < HALF - offset
    else:
        same = lane >= -offset
    return jnp.where(same, left, right), jnp.where(same, right, left)


def centre_weight(c):
    return c * ((1.0 / rate - 18.0) + c * (36.0 - 24.0 * c))


def wrap(layer):
    return lax.bitwise_and(layer, LAYERS - 1)


def halves_of(ref, layer, row, count=8):
    return tuple(ref[layer, half, row : row + count, :] for half in range(2))


def stencil(ref, layer, row, count=8):
    here = halves_of(ref, layer, row, count)
    return (
        here,
        halves_of(ref, layer + 1, row, count),
        halves_of(ref, layer - 1, row, count),
        halves_of(ref, layer, row + 1, count),
        halves_of(ref, layer, row - 1, count),
        along(here, 1),
        along(here, -1),
    )


def six(parts):
    return (parts[0] + parts[1]) + (parts[2] + parts[3]) + (parts[4] + parts[5])


def plus(total, part):
    return part if total is None else total + part


def class_sums(labels, weights):
    square = None
    cube = None
    count = len(labels)
    for i in range(count):
        rest = None
        for j in range(i + 1, count):
            rest = plus(rest, jnp.where(labels[i] == labels[j], weights[j], 0.0))
        if rest is None:
            part2 = weights[i] * weights[i]
            part3 = part2 * weights[i]
        else:
            total = rest + weights[i]
            both = total + rest
            part2 = weights[i] * both
            part3 = weights[i] * (both * both - total * rest)
        square = plus(square, part2)
        cube = plus(cube, part3)
    return square, cube


def chunks(low, high, body, group):
    count = high - low
    while count % group:
        group -= 1

    def step(index, carry):
        for k in range(group):
            body(low + index * group + k)
        return carry

    lax.fori_loop(0, count // group, step, 0)


def close_ends(ref, rows):
    ref[0, :, rows, :] = ref[LAYERS, :, rows, :]
    ref[LAYERS + 1, :, rows, :] = ref[1, :, rows, :]


def kernel(
    where_ref,
    labels_ref,
    dens_ref,
    near_ref,
    far_ref,
    grains_ref,
    out_ref,
    lab,
    c0,
    c1,
    cx,
    mu,
    k1,
    s2,
    k2,
    lab_copies,
    c_copies,
    w_copies,
    eta_mid,
    eta_edge,
):
    grain = where_ref[0]
    core = lax.rem(grain, 2)
    start = 2 * grain - TILE + LAYERS

    def place(layer):
        z = wrap(start + layer)

        def put(ref, row, value):
            for half in range(2):
                ref[layer, half, row : row + 8, :] = value[:, half * HALF : (half + 1) * HALF]

        put(lab, MID, labels_ref[z].astype(jnp.float32))
        put(c0, MID, dens_ref[z])
        for which, ref in ((0, lab), (1, c0)):
            for block in (0, 1):
                mine = near_ref[which, block, z]
                other = far_ref[which, block, z]
                put(ref, MID + 8 * (block + 1), jnp.where(core == 0, mine, other))
                put(ref, MID - 8 * (block + 1), jnp.where(core == 0, other, mine))

    chunks(0, DEEP, place, 17)

    grain_ids = [(grain * GDEV + g).astype(jnp.float32) for g in range(GDEV)]

    def own_grains(labels, weights):
        result = []
        for g in range(GDEV):
            total = None
            for one, weight in zip(labels, weights):
                total = plus(total, jnp.where(one == grain_ids[g], weight, 0.0))
            result.append(rate * total)
        return result

    def first_sums(layer, row):
        cs = stencil(c0, layer, row)
        labs = stencil(lab, layer, row)
        for half in range(2):
            labels = [one[half] for one in labs]
            weights = [one[half] for one in cs]
            weights[0] = centre_weight(weights[0])
            square, cube = class_sums(labels, weights)
            square = (rate * rate) * square
            k1[layer, half, row : row + 8, :] = (4.0 * rate**3) * cube - 6.0 * square
            if abs(row - MID) < 16:
                s2[layer, half, row : row + 8, :] = square
            if row == MID:
                for g, value in enumerate(own_grains(labels, weights)):
                    eta_mid[layer, half, 8 * g : 8 * g + 8, :] = value

    def sums_all(layer):
        for row in (MID - 8, MID, MID + 8):
            first_sums(layer, row)

    def sums_far(layer):
        for row in (MID - 16, MID + 16):
            first_sums(layer, row)

    chunks(1, LAYERS + 1, sums_all, 2)
    close_ends(eta_mid, slice(0, 8 * GDEV))
    chunks(TILE - 6, TILE + 8, sums_far, 2)

    sub = lax.broadcasted_iota(jnp.int32, (8, HALF), 0)
    upper = sub < 4

    def edge_stencil(ref, layer):
        def both(z, offset):
            high = halves_of(ref, z, MID + 8 + offset)
            low = halves_of(ref, z, MID - 8 + offset)
            return tuple(jnp.where(upper, h, w) for h, w in zip(high, low))

        here = both(layer, 0)
        return (
            here,
            both(layer + 1, 0),
            both(layer - 1, 0),
            both(layer, 1),
            both(layer, -1),
            along(here, 1),
            along(here, -1),
        )

    def edge_grains(layer):
        cs = edge_stencil(c0, layer)
        labs = edge_stencil(lab, layer)
        for half in range(2):
            weights = [one[half] for one in cs]
            weights[0] = centre_weight(weights[0])
            for g, value in enumerate(own_grains([one[half] for one in labs], weights)):
                eta_edge[layer, half, 8 * g : 8 * g + 8, :] = value

    chunks(1, LAYERS + 1, edge_grains, 4)

    def mu_at(source, extra, layer, row):
        cs = stencil(source, layer, row)
        for half in range(2):
            c = cs[0][half]
            bulk = c * (24.0 + c * (32.0 * c - 48.0)) + extra[layer, half, row : row + 8, :]
            mu[layer, half, row : row + 8, :] = bulk - six([one[half] for one in cs[1:]])

    def c_at(source, layer, row):
        ms = stencil(mu, layer, row)
        result = []
        for half in range(2):
            c = source[layer, half, row : row + 8, :]
            lap = six([one[half] for one in ms[1:]]) - 6.0 * ms[0][half]
            result.append(c + density_step * lap)
        return result

    def over(low, high, rows, body):
        if high > low and rows:

            def step(layer):
                for row in rows:
                    body(layer, row)

            chunks(low, high, step, GROUP if len(rows) > 1 else 2 * GROUP)

    sides = (MID - 8, MID + 8)
    fars = (MID - 16, MID + 16)

    def near_tile(distance):
        return TILE - distance, TILE + 2 + distance

    def passes(extra, source, target):
        def put_mu(layer, row):
            mu_at(source, extra, layer, row)

        def put_c(layer, row):
            for half, value in enumerate(c_at(source, layer, row)):
                target[layer, half, row : row + 8, :] = value

        return put_mu, put_c

    near_rows = slice(MID - 8, MID + 16)
    for sub_step in range(1, NSUB + 1):
        source = c0 if sub_step == 1 else (cx, c1)[sub_step % 2]
        target = (c1, cx)[sub_step % 2]
        put_mu, put_c = passes(k1, source, target)
        over(1, LAYERS + 1, (MID,) + sides, put_mu)
        close_ends(mu, near_rows)
        if 8 - 2 * sub_step >= 0:
            over(*near_tile(8 - 2 * sub_step), fars, put_mu)
        if sub_step < NSUB:
            over(1, LAYERS + 1, (MID,) + sides, put_c)
            close_ends(target, near_rows)
            if 7 - 2 * sub_step >= 0:
                over(*near_tile(7 - 2 * sub_step), fars, put_c)
        else:
            over(1, LAYERS + 1, (MID,), put_c)
            over(*near_tile(7), sides, put_c)

    def grain_steps(layer):
        cs = halves_of(c1, layer, MID)
        squares = halves_of(s2, layer, MID)
        linear = [
            1.0 - rate * (12.0 * (1.0 - c) + 12.0 * square + 6.0) for c, square in zip(cs, squares)
        ]
        quadratic = [(12.0 * rate) * (2.0 - c) for c in cs]
        z = wrap(start + layer)
        for g in range(GDEV):
            mid = halves_of(eta_mid, layer, 8 * g)
            edge = halves_of(eta_edge, layer, 8 * g)
            up = halves_of(eta_mid, layer + 1, 8 * g)
            down = halves_of(eta_mid, layer - 1, 8 * g)
            right = along(mid, 1)
            left = along(mid, -1)
            for half in range(2):
                here = mid[half]
                after = rolled(jnp.where(sub == 0, edge[half], here), 1, 0)
                before = rolled(jnp.where(sub == 7, edge[half], here), -1, 0)
                around = six((up[half], down[half], after, before, right[half], left[half]))
                grains_ref[g, z, :, half * HALF : (half + 1) * HALF] = (
                    here * (linear[half] + quadratic[half] * here) + rate * around
                )

    chunks(1, LAYERS + 1, grain_steps, 8)

    def copies(index):
        layer = index + BASE
        for base, count in ((MID - 16, 16), (MID, 16), (MID + 16, 8)):
            c_here = halves_of(c0, layer, base, count)
            lab_here = halves_of(lab, layer, base, count)
            for dy in range(-2, 3):
                c_cols = along(c_here, dy) if dy else c_here
                lab_cols = along(lab_here, dy) if dy else lab_here
                rows = slice(base - MID + 16, base - MID + 16 + count)
                for half in range(2):
                    c_copies[dy + 2, index, half, rows, :] = c_cols[half]
                    lab_copies[dy + 2, index, half, rows, :] = lab_cols[half]
                    if abs(dy) < 2:
                        w_copies[dy + 1, index, half, rows, :] = centre_weight(c_cols[half])

    chunks(0, 20, copies, 5)

    def second_sums(load, c, square):
        labels = [load(lab_copies, 2, cell) for cell in INNER + OUTER]
        weights = [load(w_copies, 1, cell) for cell in INNER]
        first = [weights[0]] + [load(c_copies, 2, cell) for cell in INNER[1:]]
        spread = [6.0 * load(c_copies, 2, INNER[0])] + weights[1:]
        for cell in OUTER:
            value = load(c_copies, 2, cell)
            if 2 not in cell and -2 not in cell:
                value = value + value
            spread.append(value)
        linear = rate - (rate * rate) * (12.0 * (1.0 - c) + 12.0 * square + 6.0)
        quadratic = (12.0 * rate**3) * (2.0 - c)
        inner = None
        outer = None
        for i in range(25):
            rest = None
            own_rest = None
            for j in range(i + 1, 25):
                same = labels[i] == labels[j]
                rest = plus(rest, jnp.where(same, spread[j], 0.0))
                if j < 7:
                    own_rest = plus(own_rest, jnp.where(same, first[j], 0.0))
            total = spread[i] if rest is None else rest + spread[i]
            if i < 7:
                own = first[i] if own_rest is None else own_rest + first[i]
                value = own * (linear + quadratic * own) + (rate * rate) * total
                inner = plus(inner, value * value * (4.0 * value - 6.0))
                value = (rate * rate) * rest
                if own_rest is not None:
                    value = own_rest * (linear + quadratic * own_rest) + value
                inner = inner - value * value * (4.0 * value - 6.0)
            else:
                both = total if rest is None else total + rest
                part = both * ((4.0 * rate * rate) * both - 6.0)
                if rest is not None:
                    part = part - (4.0 * rate * rate) * (total * rest)
                outer = plus(outer, spread[i] * part)
        return inner + (rate**4) * outer

    def load_block(layer, block, half):
        def load(ref, middle, cell):
            dz, dx, dy = cell
            row = 8 + 8 * block + dx
            return ref[dy + middle, layer - BASE + dz, half, row : row + 8, :]

        return load

    def halves(low, high, body):
        def step(index, carry):
            body(lax.div(index, 2), lax.rem(index, 2))
            return carry

        lax.fori_loop(2 * low, 2 * high, step, 0)

    def plain(block):
        row = MID - 8 + 8 * block

        def body(layer, half):
            k2[layer, half, row : row + 8, :] = second_sums(
                load_block(layer, block, half),
                c1[layer, half, row : row + 8, :],
                s2[layer, half, row : row + 8, :],
            )

        return body

    def merged(layer, half):
        high = load_block(layer, 2, half)
        low = load_block(layer, 0, half)

        def load(ref, middle, cell):
            return jnp.where(upper, high(ref, middle, cell), low(ref, middle, cell))

        def field(ref):
            return jnp.where(
                upper, ref[layer, half, MID + 8 : MID + 16, :], ref[layer, half, MID - 8 : MID, :]
            )

        value = second_sums(load, field(c1), field(s2))
        k2[layer, half, MID + 8 : MID + 16, :] = value
        k2[layer, half, MID - 8 : MID, :] = value

    halves(TILE - 7, TILE + 9, plain(1))
    halves(TILE - 2, TILE + 4, plain(0))
    halves(TILE - 2, TILE + 4, plain(2))
    halves(TILE - 6, TILE - 2, merged)
    halves(TILE + 4, TILE + 8, merged)

    for sub_step in range(1, NSUB + 1):
        source = (cx, c1)[sub_step % 2]
        target = (c1, cx)[sub_step % 2]
        put_mu, put_c = passes(k2, source, target)
        over(*near_tile(9 - 2 * sub_step), (MID,), put_mu)
        over(*near_tile(8 - 2 * sub_step), sides, put_mu)
        if sub_step < NSUB:
            over(*near_tile(8 - 2 * sub_step), (MID,), put_c)
            over(*near_tile(7 - 2 * sub_step), sides, put_c)
        else:
            for layer in (0, 1):
                for half, value in enumerate(c_at(source, TILE + layer, MID)):
                    out_ref[layer, :, half * HALF : (half + 1) * HALF] = value


def sintering(where, labels, dens, near, far):
    field = pltpu.VMEM((DEEP, 2, ROWS, HALF), jnp.float32)
    vmem = pl.BlockSpec(memory_space=pltpu.VMEM)
    return pl.pallas_call(
        kernel,
        out_shape=(
            jax.ShapeDtypeStruct((GDEV, LAYERS, 8, WIDTH), jnp.float32),
            jax.ShapeDtypeStruct((2, 8, WIDTH), jnp.float32),
        ),
        in_specs=[pl.BlockSpec(memory_space=pltpu.SMEM)] + [vmem] * 4,
        out_specs=(vmem, vmem),
        scratch_shapes=[field] * 8
        + [
            pltpu.VMEM((5, 20, 2, 40, HALF), jnp.float32),
            pltpu.VMEM((5, 20, 2, 40, HALF), jnp.float32),
            pltpu.VMEM((3, 20, 2, 40, HALF), jnp.float32),
            pltpu.VMEM((DEEP, 2, 8 * GDEV, HALF), jnp.float32),
            pltpu.VMEM((DEEP, 2, 8 * GDEV, HALF), jnp.float32),
        ],
        compiler_params=pltpu.CompilerParams(vmem_limit_bytes=56 * 1024 * 1024),
        name="sintering",
    )(where, labels, dens, near, far)


def from_sides(block, distance):
    grains = lax.axis_size("grain")
    count = lax.axis_size("space")
    pairs = []
    for g in range(grains):
        way = distance if g % 2 == 0 else -distance
        for s in range(count):
            pairs.append((g * count + (s + way) % count, g * count + s))
    return lax.ppermute(block, ("grain", "space"), pairs)


def swap_cores(block):
    return lax.ppermute(block, "grain", [(i, i ^ 1) for i in range(lax.axis_size("grain"))])


def per_device(labels, density):
    grain = lax.axis_index("grain")
    named = labels.astype(jnp.float32)
    own = jnp.broadcast_to(density[None], (lax.axis_size("grain"),) + density.shape)
    dens = lax.all_to_all(own, "grain", 0, 0).reshape(LAYERS, 8, WIDTH)
    named_sides = [from_sides(named, distance) for distance in (1, 2)]
    dens_sides = [from_sides(dens, distance) for distance in (1, 2)]
    near = jnp.stack([jnp.stack(named_sides), jnp.stack(dens_sides)])
    far = swap_cores(near)
    return sintering(grain.reshape(1).astype(jnp.int32), labels, dens, near, far)


def solution(mesh):
    return jax.shard_map(
        per_device,
        mesh=mesh,
        in_specs=(P(None, "space", None), P("grain", "space", None)),
        out_specs=(P("grain", None, "space", None), P("grain", "space", None)),
        check_vma=False,
    )
```

```python
import functools

import jax
import jax.numpy as jnp
from jax import lax
from jax.experimental import pallas as pl
from jax.experimental.pallas import tpu as pltpu
from jax.sharding import PartitionSpec as P

GDEV = 4
NSUB = 4
LAYERS = 32
DEEP = 34
WIDTH = 256
HALF = 128
ROWS = 56
MID = 24
TILE = 16
BASE = 7
GROUP = 32

rate = 0.008 * 2.0
density_step = 0.004

INNER = ((0, 0, 0), (1, 0, 0), (-1, 0, 0), (0, 1, 0), (0, -1, 0), (0, 0, 1), (0, 0, -1))
OUTER = tuple(
    (dz, dx, dy)
    for dz in range(-2, 3)
    for dx in range(-2, 3)
    for dy in range(-2, 3)
    if abs(dz) + abs(dx) + abs(dy) == 2
)


def rolled(x, offset, axis):
    size = x.shape[axis]
    return pltpu.roll(x, (-offset) % size, axis)


def along(pair, offset):
    left, right = rolled(pair[0], offset, 1), rolled(pair[1], offset, 1)
    lane = lax.broadcasted_iota(jnp.int32, left.shape, 1)
    if offset > 0:
        same = lane < HALF - offset
    else:
        same = lane >= -offset
    return jnp.where(same, left, right), jnp.where(same, right, left)


def centre_weight(c):
    return c * ((1.0 / rate - 18.0) + c * (36.0 - 24.0 * c))


def wrap(layer):
    return lax.bitwise_and(layer, LAYERS - 1)


def halves_of(ref, layer, row, count=8):
    return tuple(ref[layer, half, row : row + count, :] for half in range(2))


def stencil(ref, layer, row, count=8):
    here = halves_of(ref, layer, row, count)
    return (
        here,
        halves_of(ref, layer + 1, row, count),
        halves_of(ref, layer - 1, row, count),
        halves_of(ref, layer, row + 1, count),
        halves_of(ref, layer, row - 1, count),
        along(here, 1),
        along(here, -1),
    )


def six(parts):
    return (parts[0] + parts[1]) + (parts[2] + parts[3]) + (parts[4] + parts[5])


def plus(total, part):
    return part if total is None else total + part


def class_sums(labels, weights):
    square = None
    cube = None
    count = len(labels)
    for i in range(count):
        rest = None
        for j in range(i + 1, count):
            rest = plus(rest, jnp.where(labels[i] == labels[j], weights[j], 0.0))
        if rest is None:
            part2 = weights[i] * weights[i]
            part3 = part2 * weights[i]
        else:
            total = rest + weights[i]
            both = total + rest
            part2 = weights[i] * both
            part3 = weights[i] * (both * both - total * rest)
        square = plus(square, part2)
        cube = plus(cube, part3)
    return square, cube


def chunks(low, high, body, group):
    count = high - low
    while count % group:
        group -= 1

    def step(index, carry):
        for k in range(group):
            body(low + index * group + k)
        return carry

    lax.fori_loop(0, count // group, step, 0)


def close_ends(ref, rows):
    ref[0, :, rows, :] = ref[LAYERS, :, rows, :]
    ref[LAYERS + 1, :, rows, :] = ref[1, :, rows, :]


def kernel(
    where_ref,
    labels_ref,
    dens_ref,
    near_labels_ref,
    near_dens_ref,
    far_labels_ref,
    far_dens_ref,
    grains_out,
    out_ref,
    lab,
    c0,
    c1,
    cx,
    mu,
    k1,
    s2,
    k2,
    lab_copies,
    c_copies,
    w_copies,
    eta_mid,
    eta_edge,
    grains_ref,
    far_dens,
    sems,
):
    grain = where_ref[0]
    core = lax.rem(grain, 2)
    start = 2 * grain - TILE + LAYERS

    incoming = pltpu.make_async_copy(far_dens_ref, far_dens, sems.at[0])
    incoming.start()
    near_rows = [MID + 8 * (block + 1) * (1 - 2 * core) for block in (0, 1)]
    far_rows = [MID - 8 * (block + 1) * (1 - 2 * core) for block in (0, 1)]

    def put(ref, layer, row, value):
        for half in range(2):
            part = value[:, half * HALF : (half + 1) * HALF]
            ref[layer, half, pl.ds(pl.multiple_of(row, 8), 8), :] = part

    def place(layer):
        z = wrap(start + layer)
        put(lab, layer, MID, labels_ref[z].astype(jnp.float32))
        put(c0, layer, MID, dens_ref[z])
        for block in (0, 1):
            put(lab, layer, near_rows[block], near_labels_ref[block, z])
            put(lab, layer, far_rows[block], far_labels_ref[block, z])
            put(c0, layer, near_rows[block], near_dens_ref[block, z])

    def place_far(layer):
        z = wrap(start + layer)
        for block in (0, 1):
            put(c0, layer, far_rows[block], far_dens[block, z])

    chunks(0, DEEP, place, 17)
    incoming.wait()
    chunks(0, DEEP, place_far, 17)

    grain_ids = [(grain * GDEV + g).astype(jnp.float32) for g in range(GDEV)]

    def own_grains(labels, weights):
        result = []
        for g in range(GDEV):
            total = None
            for one, weight in zip(labels, weights):
                total = plus(total, jnp.where(one == grain_ids[g], weight, 0.0))
            result.append(rate * total)
        return result

    def first_sums(layer, row):
        cs = stencil(c0, layer, row)
        labs = stencil(lab, layer, row)
        for half in range(2):
            labels = [one[half] for one in labs]
            weights = [one[half] for one in cs]
            weights[0] = centre_weight(weights[0])
            square, cube = class_sums(labels, weights)
            square = (rate * rate) * square
            k1[layer, half, row : row + 8, :] = (4.0 * rate**3) * cube - 6.0 * square
            if abs(row - MID) < 16:
                s2[layer, half, row : row + 8, :] = square
            if row == MID:
                for g, value in enumerate(own_grains(labels, weights)):
                    eta_mid[layer, half, 8 * g : 8 * g + 8, :] = value

    def sums_all(layer):
        for row in (MID - 8, MID, MID + 8):
            first_sums(layer, row)

    def sums_far(layer):
        for row in (MID - 16, MID + 16):
            first_sums(layer, row)

    chunks(1, LAYERS + 1, sums_all, 2)
    close_ends(eta_mid, slice(0, 8 * GDEV))
    chunks(TILE - 6, TILE + 8, sums_far, 2)

    sub = lax.broadcasted_iota(jnp.int32, (8, HALF), 0)
    upper = sub < 4

    def edge_stencil(ref, layer):
        def both(z, offset):
            high = halves_of(ref, z, MID + 8 + offset)
            low = halves_of(ref, z, MID - 8 + offset)
            return tuple(jnp.where(upper, h, w) for h, w in zip(high, low))

        here = both(layer, 0)
        return (
            here,
            both(layer + 1, 0),
            both(layer - 1, 0),
            both(layer, 1),
            both(layer, -1),
            along(here, 1),
            along(here, -1),
        )

    def edge_grains(layer):
        cs = edge_stencil(c0, layer)
        labs = edge_stencil(lab, layer)
        for half in range(2):
            weights = [one[half] for one in cs]
            weights[0] = centre_weight(weights[0])
            for g, value in enumerate(own_grains([one[half] for one in labs], weights)):
                eta_edge[layer, half, 8 * g : 8 * g + 8, :] = value

    chunks(1, LAYERS + 1, edge_grains, 4)

    def mu_at(source, extra, layer, row):
        cs = stencil(source, layer, row)
        for half in range(2):
            c = cs[0][half]
            bulk = c * (24.0 + c * (32.0 * c - 48.0)) + extra[layer, half, row : row + 8, :]
            mu[layer, half, row : row + 8, :] = bulk - six([one[half] for one in cs[1:]])

    def c_at(source, layer, row):
        ms = stencil(mu, layer, row)
        result = []
        for half in range(2):
            c = source[layer, half, row : row + 8, :]
            lap = six([one[half] for one in ms[1:]]) - 6.0 * ms[0][half]
            result.append(c + density_step * lap)
        return result

    def over(low, high, rows, body):
        if high > low and rows:

            def step(layer):
                for row in rows:
                    body(layer, row)

            chunks(low, high, step, GROUP if len(rows) > 1 else 2 * GROUP)

    sides = (MID - 8, MID + 8)
    fars = (MID - 16, MID + 16)

    def near_tile(distance):
        return TILE - distance, TILE + 2 + distance

    def passes(extra, source, target):
        def put_mu(layer, row):
            mu_at(source, extra, layer, row)

        def put_c(layer, row):
            for half, value in enumerate(c_at(source, layer, row)):
                target[layer, half, row : row + 8, :] = value

        return put_mu, put_c

    span = slice(MID - 8, MID + 16)
    for sub_step in range(1, NSUB + 1):
        source = c0 if sub_step == 1 else (cx, c1)[sub_step % 2]
        target = (c1, cx)[sub_step % 2]
        put_mu, put_c = passes(k1, source, target)
        over(1, LAYERS + 1, (MID,) + sides, put_mu)
        close_ends(mu, span)
        if 8 - 2 * sub_step >= 0:
            over(*near_tile(8 - 2 * sub_step), fars, put_mu)
        if sub_step < NSUB:
            over(1, LAYERS + 1, (MID,) + sides, put_c)
            close_ends(target, span)
            if 7 - 2 * sub_step >= 0:
                over(*near_tile(7 - 2 * sub_step), fars, put_c)
        else:
            over(1, LAYERS + 1, (MID,), put_c)
            over(*near_tile(7), sides, put_c)

    def grain_steps(layer):
        cs = halves_of(c1, layer, MID)
        squares = halves_of(s2, layer, MID)
        linear = [
            1.0 - rate * (12.0 * (1.0 - c) + 12.0 * square + 6.0) for c, square in zip(cs, squares)
        ]
        quadratic = [(12.0 * rate) * (2.0 - c) for c in cs]
        z = wrap(start + layer)
        for g in range(GDEV):
            mid = halves_of(eta_mid, layer, 8 * g)
            edge = halves_of(eta_edge, layer, 8 * g)
            up = halves_of(eta_mid, layer + 1, 8 * g)
            down = halves_of(eta_mid, layer - 1, 8 * g)
            right = along(mid, 1)
            left = along(mid, -1)
            for half in range(2):
                here = mid[half]
                after = rolled(jnp.where(sub == 0, edge[half], here), 1, 0)
                before = rolled(jnp.where(sub == 7, edge[half], here), -1, 0)
                around = six((up[half], down[half], after, before, right[half], left[half]))
                grains_ref[g, z, :, half * HALF : (half + 1) * HALF] = (
                    here * (linear[half] + quadratic[half] * here) + rate * around
                )

    chunks(1, LAYERS + 1, grain_steps, 8)
    outgoing = pltpu.make_async_copy(grains_ref, grains_out, sems.at[1])
    outgoing.start()

    def copies(index):
        layer = index + BASE
        for base, count in ((MID - 16, 16), (MID, 16), (MID + 16, 8)):
            c_here = halves_of(c0, layer, base, count)
            lab_here = halves_of(lab, layer, base, count)
            for dy in range(-2, 3):
                c_cols = along(c_here, dy) if dy else c_here
                lab_cols = along(lab_here, dy) if dy else lab_here
                rows = slice(base - MID + 16, base - MID + 16 + count)
                for half in range(2):
                    c_copies[dy + 2, index, half, rows, :] = c_cols[half]
                    lab_copies[dy + 2, index, half, rows, :] = lab_cols[half]
                    if abs(dy) < 2:
                        w_copies[dy + 1, index, half, rows, :] = centre_weight(c_cols[half])

    chunks(0, 20, copies, 5)

    def second_sums(load, c, square):
        labels = [load(lab_copies, 2, cell) for cell in INNER + OUTER]
        weights = [load(w_copies, 1, cell) for cell in INNER]
        first = [weights[0]] + [load(c_copies, 2, cell) for cell in INNER[1:]]
        spread = [6.0 * load(c_copies, 2, INNER[0])] + weights[1:]
        for cell in OUTER:
            value = load(c_copies, 2, cell)
            if 2 not in cell and -2 not in cell:
                value = value + value
            spread.append(value)
        linear = rate - (rate * rate) * (12.0 * (1.0 - c) + 12.0 * square + 6.0)
        quadratic = (12.0 * rate**3) * (2.0 - c)
        inner = None
        outer = None
        for i in range(25):
            rest = None
            own_rest = None
            for j in range(i + 1, 25):
                same = labels[i] == labels[j]
                rest = plus(rest, jnp.where(same, spread[j], 0.0))
                if j < 7:
                    own_rest = plus(own_rest, jnp.where(same, first[j], 0.0))
            total = spread[i] if rest is None else rest + spread[i]
            if i < 7:
                own = first[i] if own_rest is None else own_rest + first[i]
                value = own * (linear + quadratic * own) + (rate * rate) * total
                inner = plus(inner, value * value * (4.0 * value - 6.0))
                value = (rate * rate) * rest
                if own_rest is not None:
                    value = own_rest * (linear + quadratic * own_rest) + value
                inner = inner - value * value * (4.0 * value - 6.0)
            else:
                both = total if rest is None else total + rest
                part = both * ((4.0 * rate * rate) * both - 6.0)
                if rest is not None:
                    part = part - (4.0 * rate * rate) * (total * rest)
                outer = plus(outer, spread[i] * part)
        return inner + (rate**4) * outer

    def load_block(layer, block, half):
        def load(ref, middle, cell):
            dz, dx, dy = cell
            row = 8 + 8 * block + dx
            return ref[dy + middle, layer - BASE + dz, half, row : row + 8, :]

        return load

    def halves(low, high, body):
        def step(index, carry):
            body(lax.div(index, 2), lax.rem(index, 2))
            return carry

        lax.fori_loop(2 * low, 2 * high, step, 0)

    def plain(block):
        row = MID - 8 + 8 * block

        def body(layer, half):
            k2[layer, half, row : row + 8, :] = second_sums(
                load_block(layer, block, half),
                c1[layer, half, row : row + 8, :],
                s2[layer, half, row : row + 8, :],
            )

        return body

    def merged(layer, half):
        high = load_block(layer, 2, half)
        low = load_block(layer, 0, half)

        def load(ref, middle, cell):
            return jnp.where(upper, high(ref, middle, cell), low(ref, middle, cell))

        def field(ref):
            return jnp.where(
                upper, ref[layer, half, MID + 8 : MID + 16, :], ref[layer, half, MID - 8 : MID, :]
            )

        value = second_sums(load, field(c1), field(s2))
        k2[layer, half, MID + 8 : MID + 16, :] = value
        k2[layer, half, MID - 8 : MID, :] = value

    halves(TILE - 7, TILE + 9, plain(1))
    halves(TILE - 2, TILE + 4, plain(0))
    halves(TILE - 2, TILE + 4, plain(2))
    halves(TILE - 6, TILE - 2, merged)
    halves(TILE + 4, TILE + 8, merged)

    for sub_step in range(1, NSUB + 1):
        source = (cx, c1)[sub_step % 2]
        target = (c1, cx)[sub_step % 2]
        put_mu, put_c = passes(k2, source, target)
        over(*near_tile(9 - 2 * sub_step), (MID,), put_mu)
        over(*near_tile(8 - 2 * sub_step), sides, put_mu)
        if sub_step < NSUB:
            over(*near_tile(8 - 2 * sub_step), (MID,), put_c)
            over(*near_tile(7 - 2 * sub_step), sides, put_c)
        else:
            for layer in (0, 1):
                for half, value in enumerate(c_at(source, TILE + layer, MID)):
                    out_ref[layer, :, half * HALF : (half + 1) * HALF] = value
    outgoing.wait()


def sintering(where, labels, dens, near_labels, near_dens, far_labels, far_dens):
    field = pltpu.VMEM((DEEP, 2, ROWS, HALF), jnp.float32)
    vmem = pl.BlockSpec(memory_space=pltpu.VMEM)
    anywhere = pl.BlockSpec(memory_space=pl.ANY)
    return pl.pallas_call(
        kernel,
        out_shape=(
            jax.ShapeDtypeStruct((GDEV, LAYERS, 8, WIDTH), jnp.float32),
            jax.ShapeDtypeStruct((2, 8, WIDTH), jnp.float32),
        ),
        in_specs=[pl.BlockSpec(memory_space=pltpu.SMEM)] + [vmem] * 5 + [anywhere],
        out_specs=(anywhere, vmem),
        scratch_shapes=[field] * 8
        + [
            pltpu.VMEM((5, 20, 2, 40, HALF), jnp.float32),
            pltpu.VMEM((5, 20, 2, 40, HALF), jnp.float32),
            pltpu.VMEM((3, 20, 2, 40, HALF), jnp.float32),
            pltpu.VMEM((DEEP, 2, 8 * GDEV, HALF), jnp.float32),
            pltpu.VMEM((DEEP, 2, 8 * GDEV, HALF), jnp.float32),
            pltpu.VMEM((GDEV, LAYERS, 8, WIDTH), jnp.float32),
            pltpu.VMEM((2, LAYERS, 8, WIDTH), jnp.float32),
            pltpu.SemaphoreType.DMA((2,)),
        ],
        compiler_params=pltpu.CompilerParams(vmem_limit_bytes=56 * 1024 * 1024),
        name="sintering",
    )(where, labels, dens, near_labels, near_dens, far_labels, far_dens)


def from_sides(block, distance):
    grains = lax.axis_size("grain")
    count = lax.axis_size("space")
    pairs = []
    for g in range(grains):
        way = distance if g % 2 == 0 else -distance
        for s in range(count):
            pairs.append((g * count + (s + way) % count, g * count + s))
    return lax.ppermute(block, ("grain", "space"), pairs)


def swap_cores(block):
    return lax.ppermute(block, "grain", [(i, i ^ 1) for i in range(lax.axis_size("grain"))])


def per_device(labels, density):
    grain = lax.axis_index("grain")
    named = labels.astype(jnp.float32)
    own = jnp.broadcast_to(density[None], (lax.axis_size("grain"),) + density.shape)
    dens = lax.all_to_all(own, "grain", 0, 0).reshape(LAYERS, 8, WIDTH)
    far_side, near_side = [from_sides(named, distance) for distance in (2, 1)]
    near_labels = jnp.stack([near_side, far_side])
    far_side, near_side = [from_sides(dens, distance) for distance in (2, 1)]
    near_dens = jnp.stack([near_side, far_side])
    far_labels = swap_cores(near_labels)
    far_dens = swap_cores(near_dens)
    return sintering(
        grain.reshape(1).astype(jnp.int32),
        labels,
        dens,
        near_labels,
        near_dens,
        far_labels,
        far_dens,
    )


def solution(mesh):
    return jax.shard_map(
        per_device,
        mesh=mesh,
        in_specs=(P(None, "space", None), P("grain", "space", None)),
        out_specs=(P("grain", None, "space", None), P("grain", "space", None)),
        check_vma=False,
    )
```

```python
import functools

import jax
import jax.numpy as jnp
from jax import lax
from jax.experimental import pallas as pl
from jax.experimental.pallas import tpu as pltpu
from jax.sharding import PartitionSpec as P

GDEV = 4
NSUB = 4
LAYERS = 32
DEEP = 34
WIDTH = 256
HALF = 128
ROWS = 56
MID = 24
TILE = 16
BASE = 7
GROUP = 32

rate = 0.008 * 2.0
density_step = 0.004

INNER = ((0, 0, 0), (1, 0, 0), (-1, 0, 0), (0, 1, 0), (0, -1, 0), (0, 0, 1), (0, 0, -1))
OUTER = tuple(
    (dz, dx, dy)
    for dz in range(-2, 3)
    for dx in range(-2, 3)
    for dy in range(-2, 3)
    if abs(dz) + abs(dx) + abs(dy) == 2
)


def rolled(x, offset, axis):
    size = x.shape[axis]
    return pltpu.roll(x, (-offset) % size, axis)


def along(pair, offset):
    left, right = rolled(pair[0], offset, 1), rolled(pair[1], offset, 1)
    lane = lax.broadcasted_iota(jnp.int32, left.shape, 1)
    if offset > 0:
        same = lane < HALF - offset
    else:
        same = lane >= -offset
    return jnp.where(same, left, right), jnp.where(same, right, left)


def centre_weight(c):
    return c * ((1.0 / rate - 18.0) + c * (36.0 - 24.0 * c))


def wrap(layer):
    return lax.bitwise_and(layer, LAYERS - 1)


def halves_of(ref, layer, row, count=8):
    return tuple(ref[layer, half, row : row + count, :] for half in range(2))


def stencil(ref, layer, row, count=8):
    here = halves_of(ref, layer, row, count)
    return (
        here,
        halves_of(ref, layer + 1, row, count),
        halves_of(ref, layer - 1, row, count),
        halves_of(ref, layer, row + 1, count),
        halves_of(ref, layer, row - 1, count),
        along(here, 1),
        along(here, -1),
    )


def six(parts):
    return (parts[0] + parts[1]) + (parts[2] + parts[3]) + (parts[4] + parts[5])


def plus(total, part):
    return part if total is None else total + part


def class_sums(labels, weights):
    square = None
    cube = None
    count = len(labels)
    for i in range(count):
        rest = None
        for j in range(i + 1, count):
            rest = plus(rest, jnp.where(labels[i] == labels[j], weights[j], 0.0))
        if rest is None:
            part2 = weights[i] * weights[i]
            part3 = part2 * weights[i]
        else:
            total = rest + weights[i]
            both = total + rest
            part2 = weights[i] * both
            part3 = weights[i] * (both * both - total * rest)
        square = plus(square, part2)
        cube = plus(cube, part3)
    return square, cube


def chunks(low, high, body, group):
    count = high - low
    while count % group:
        group -= 1

    def step(index, carry):
        for k in range(group):
            body(low + index * group + k)
        return carry

    lax.fori_loop(0, count // group, step, 0)


def close_ends(ref, rows):
    ref[0, :, rows, :] = ref[LAYERS, :, rows, :]
    ref[LAYERS + 1, :, rows, :] = ref[1, :, rows, :]


def kernel(
    where_ref,
    labels_ref,
    dens_ref,
    near_labels_ref,
    near_dens_ref,
    far_labels_ref,
    far_dens_ref,
    grains_out,
    out_ref,
    lab,
    c0,
    c1,
    cx,
    mu,
    k1,
    s2,
    k2,
    lab_copies,
    c_copies,
    w_copies,
    eta_mid,
    eta_edge,
    grains_ref,
    far_dens,
    triples,
    sems,
):
    grain = where_ref[0]
    core = lax.rem(grain, 2)
    start = 2 * grain - TILE + LAYERS

    incoming = pltpu.make_async_copy(far_dens_ref, far_dens, sems.at[0])
    incoming.start()
    near_rows = [MID + 8 * (block + 1) * (1 - 2 * core) for block in (0, 1)]
    far_rows = [MID - 8 * (block + 1) * (1 - 2 * core) for block in (0, 1)]

    def put(ref, layer, row, value):
        for half in range(2):
            part = value[:, half * HALF : (half + 1) * HALF]
            ref[layer, half, pl.ds(pl.multiple_of(row, 8), 8), :] = part

    def place(layer):
        z = wrap(start + layer)
        put(lab, layer, MID, labels_ref[z].astype(jnp.float32))
        put(c0, layer, MID, dens_ref[z])
        for block in (0, 1):
            put(lab, layer, near_rows[block], near_labels_ref[block, z])
            put(lab, layer, far_rows[block], far_labels_ref[block, z])
            put(c0, layer, near_rows[block], near_dens_ref[block, z])

    def place_far(layer):
        z = wrap(start + layer)
        for block in (0, 1):
            put(c0, layer, far_rows[block], far_dens[block, z])

    chunks(0, DEEP, place, 17)
    incoming.wait()
    chunks(0, DEEP, place_far, 17)

    grain_ids = [(grain * GDEV + g).astype(jnp.float32) for g in range(GDEV)]

    def own_grains(labels, weights):
        result = []
        for g in range(GDEV):
            total = None
            for one, weight in zip(labels, weights):
                total = plus(total, jnp.where(one == grain_ids[g], weight, 0.0))
            result.append(rate * total)
        return result

    def first_sums(layer, row):
        cs = stencil(c0, layer, row)
        labs = stencil(lab, layer, row)
        for half in range(2):
            labels = [one[half] for one in labs]
            weights = [one[half] for one in cs]
            weights[0] = centre_weight(weights[0])
            square, cube = class_sums(labels, weights)
            square = (rate * rate) * square
            k1[layer, half, row : row + 8, :] = (4.0 * rate**3) * cube - 6.0 * square
            if abs(row - MID) < 16:
                s2[layer, half, row : row + 8, :] = square
            if row == MID:
                for g, value in enumerate(own_grains(labels, weights)):
                    eta_mid[layer, half, 8 * g : 8 * g + 8, :] = value

    def sums_all(layer):
        for row in (MID - 8, MID, MID + 8):
            first_sums(layer, row)

    def sums_far(layer):
        for row in (MID - 16, MID + 16):
            first_sums(layer, row)

    chunks(1, LAYERS + 1, sums_all, 2)
    close_ends(eta_mid, slice(0, 8 * GDEV))
    chunks(TILE - 6, TILE + 8, sums_far, 2)

    sub = lax.broadcasted_iota(jnp.int32, (8, HALF), 0)
    upper = sub < 4

    def edge_stencil(ref, layer):
        def both(z, offset):
            high = halves_of(ref, z, MID + 8 + offset)
            low = halves_of(ref, z, MID - 8 + offset)
            return tuple(jnp.where(upper, h, w) for h, w in zip(high, low))

        here = both(layer, 0)
        return (
            here,
            both(layer + 1, 0),
            both(layer - 1, 0),
            both(layer, 1),
            both(layer, -1),
            along(here, 1),
            along(here, -1),
        )

    def edge_grains(layer):
        cs = edge_stencil(c0, layer)
        labs = edge_stencil(lab, layer)
        for half in range(2):
            weights = [one[half] for one in cs]
            weights[0] = centre_weight(weights[0])
            for g, value in enumerate(own_grains([one[half] for one in labs], weights)):
                eta_edge[layer, half, 8 * g : 8 * g + 8, :] = value

    chunks(1, LAYERS + 1, edge_grains, 4)

    def mu_at(source, extra, layer, row):
        cs = stencil(source, layer, row)
        for half in range(2):
            c = cs[0][half]
            bulk = c * (24.0 + c * (32.0 * c - 48.0)) + extra[layer, half, row : row + 8, :]
            mu[layer, half, row : row + 8, :] = bulk - six([one[half] for one in cs[1:]])

    def c_at(source, layer, row):
        ms = stencil(mu, layer, row)
        result = []
        for half in range(2):
            c = source[layer, half, row : row + 8, :]
            lap = six([one[half] for one in ms[1:]]) - 6.0 * ms[0][half]
            result.append(c + density_step * lap)
        return result

    def over(low, high, rows, body):
        if high > low and rows:

            def step(layer):
                for row in rows:
                    body(layer, row)

            chunks(low, high, step, GROUP if len(rows) > 1 else 2 * GROUP)

    sides = (MID - 8, MID + 8)
    fars = (MID - 16, MID + 16)

    def near_tile(distance):
        return TILE - distance, TILE + 2 + distance

    def passes(extra, source, target):
        def put_mu(layer, row):
            mu_at(source, extra, layer, row)

        def put_c(layer, row):
            for half, value in enumerate(c_at(source, layer, row)):
                target[layer, half, row : row + 8, :] = value

        return put_mu, put_c

    span = slice(MID - 8, MID + 16)
    for sub_step in range(1, NSUB + 1):
        source = c0 if sub_step == 1 else (cx, c1)[sub_step % 2]
        target = (c1, cx)[sub_step % 2]
        put_mu, put_c = passes(k1, source, target)
        over(1, LAYERS + 1, (MID,) + sides, put_mu)
        close_ends(mu, span)
        if 8 - 2 * sub_step >= 0:
            over(*near_tile(8 - 2 * sub_step), fars, put_mu)
        if sub_step < NSUB:
            over(1, LAYERS + 1, (MID,) + sides, put_c)
            close_ends(target, span)
            if 7 - 2 * sub_step >= 0:
                over(*near_tile(7 - 2 * sub_step), fars, put_c)
        else:
            over(1, LAYERS + 1, (MID,), put_c)
            over(*near_tile(7), sides, put_c)

    def grain_steps(layer):
        cs = halves_of(c1, layer, MID)
        squares = halves_of(s2, layer, MID)
        linear = [
            1.0 - rate * (12.0 * (1.0 - c) + 12.0 * square + 6.0) for c, square in zip(cs, squares)
        ]
        quadratic = [(12.0 * rate) * (2.0 - c) for c in cs]
        z = wrap(start + layer)
        for g in range(GDEV):
            mid = halves_of(eta_mid, layer, 8 * g)
            edge = halves_of(eta_edge, layer, 8 * g)
            up = halves_of(eta_mid, layer + 1, 8 * g)
            down = halves_of(eta_mid, layer - 1, 8 * g)
            right = along(mid, 1)
            left = along(mid, -1)
            for half in range(2):
                here = mid[half]
                after = rolled(jnp.where(sub == 0, edge[half], here), 1, 0)
                before = rolled(jnp.where(sub == 7, edge[half], here), -1, 0)
                around = six((up[half], down[half], after, before, right[half], left[half]))
                grains_ref[g, z, :, half * HALF : (half + 1) * HALF] = (
                    here * (linear[half] + quadratic[half] * here) + rate * around
                )

    chunks(1, LAYERS + 1, grain_steps, 8)
    outgoing = pltpu.make_async_copy(grains_ref, grains_out, sems.at[1])
    outgoing.start()

    def copies(index):
        layer = index + BASE
        for base, count in ((MID - 16, 16), (MID, 16), (MID + 16, 8)):
            c_here = halves_of(c0, layer, base, count)
            lab_here = halves_of(lab, layer, base, count)
            for dy in range(-2, 3):
                c_cols = along(c_here, dy) if dy else c_here
                lab_cols = along(lab_here, dy) if dy else lab_here
                rows = slice(base - MID + 16, base - MID + 16 + count)
                for half in range(2):
                    c_copies[dy + 2, index, half, rows, :] = c_cols[half]
                    lab_copies[dy + 2, index, half, rows, :] = lab_cols[half]
                    if abs(dy) < 2:
                        w_copies[dy + 1, index, half, rows, :] = centre_weight(c_cols[half])

    chunks(0, 20, copies, 5)

    odd = lax.rem(sub, 2) == 1
    lane = lax.broadcasted_iota(jnp.int32, (8, HALF), 1)
    early = lax.rem(lane, 8) < 4

    def swapped(value, step):
        bit = lax.rem(lax.div(lane, step), 2) == 1
        return jnp.where(bit, rolled(value, -step, 1), rolled(value, step, 1))

    def block_labels(pair):
        for block in range(3):
            row = MID - 8 + 8 * block
            for half in range(2):
                cells = []
                for layer in (2 * pair, 2 * pair + 1):
                    cells.append(lab[layer, half, row : row + 8, :])
                    after = lab[layer, half, row + 1 : row + 9, :]
                    before = lab[layer, half, row - 1 : row + 7, :]
                    cells.append(jnp.where(odd, before, after))

                def over_block(pick, values):
                    result = pick(pick(values[0], values[1]), pick(values[2], values[3]))
                    for step in (1, 2, 4):
                        result = pick(result, swapped(result, step))
                    return result

                high = over_block(jnp.maximum, cells)
                low = over_block(jnp.minimum, cells)
                others = [
                    jnp.where(cell == high, -1.0, jnp.where(cell == low, -1.0, cell))
                    for cell in cells
                ]
                middle = over_block(jnp.maximum, others)
                low = jnp.where(low == high, -1.0, low)
                for slot, value in enumerate((high, middle, low)):
                    triples[slot, pair - 4, half, 8 * block : 8 * block + 8, :] = value

    chunks(4, 13, block_labels, 3)

    def second_sums(load, own_labels, c, square, out):
        labels = {cell: load(lab_copies, 2, cell) for cell in INNER + OUTER}
        spread = {cell: load(w_copies, 1, cell) for cell in INNER}
        first = {cell: load(c_copies, 2, cell) for cell in INNER}
        spread[INNER[0]], first[INNER[0]] = 6.0 * first[INNER[0]], spread[INNER[0]]
        for cell in OUTER:
            value = load(c_copies, 2, cell)
            spread[cell] = value if 2 in cell or -2 in cell else value + value
        linear = rate - (rate * rate) * (12.0 * (1.0 - c) + 12.0 * square + 6.0)
        quadratic = (12.0 * rate**3) * (2.0 - c)

        def settled(own, total):
            value = (rate * rate) * total
            if own is not None:
                value = own * (linear + quadratic * own) + value
            return value * value * (4.0 * value - 6.0)

        taken = {}
        taken_first = {}
        inner = None
        for one in own_labels:
            total = None
            own = None
            for cell in INNER + OUTER:
                same = labels[cell] == one
                part = jnp.where(same, spread[cell], 0.0)
                total = plus(total, part)
                taken[cell] = plus(taken.get(cell), part)
                if cell in first:
                    part = jnp.where(same, first[cell], 0.0)
                    own = plus(own, part)
                    taken_first[cell] = plus(taken_first.get(cell), part)
            inner = plus(inner, settled(own, total))
        left = {cell: spread[cell] - taken[cell] for cell in INNER[1:] + OUTER}
        left_first = {cell: first[cell] - taken_first[cell] for cell in INNER[1:]}

        def by(mask, one, two):
            return (
                jnp.where(mask, labels[one], labels[two]),
                left[one] + left[two],
                left_first[one] + left_first[two] if one in left_first else None,
            )

        def alone(cell):
            return labels[cell], left[cell], left_first.get(cell)

        slots = [
            alone((out, 0, 0)),
            by(odd, (0, 1, 0), (0, -1, 0)),
            by(early, (0, 0, -1), (0, 0, 1)),
            alone((2, 0, 0)),
            alone((-2, 0, 0)),
            alone((out, 0, 1)),
            alone((out, 0, -1)),
            alone((out, 1, 0)),
            alone((out, -1, 0)),
            by(odd, (-out, 1, 0), (-out, -1, 0)),
            by(early, (-out, 0, -1), (-out, 0, 1)),
            alone((0, 2, 0)),
            alone((0, -2, 0)),
            by(early, (0, 0, -2), (0, 0, 2)),
        ]
        turned = {}
        for dy in (-1, 1):
            one, two = (0, 1, dy), (0, -1, dy)
            slots.append(
                (
                    jnp.where(odd, labels[one], labels[two]),
                    jnp.where(odd, left[one], left[two]),
                    None,
                )
            )
            turned[dy] = (
                jnp.where(odd, labels[two], labels[one]),
                jnp.where(odd, left[two], left[one]),
            )
        slots.append(
            (jnp.where(early, turned[-1][0], turned[1][0]), turned[-1][1] + turned[1][1], None)
        )

        outer = None
        for i, (label, weight, weight_first) in enumerate(slots):
            rest = None
            own_rest = None
            for other, value, value_first in slots[i + 1 :]:
                same = label == other
                rest = plus(rest, jnp.where(same, value, 0.0))
                if value_first is not None:
                    own_rest = plus(own_rest, jnp.where(same, value_first, 0.0))
            if weight_first is not None:
                own = weight_first if own_rest is None else own_rest + weight_first
                inner = inner + settled(own, rest + weight) - settled(own_rest, rest)
            else:
                total = weight if rest is None else rest + weight
                both = total if rest is None else total + rest
                part = both * ((4.0 * rate * rate) * both - 6.0)
                if rest is not None:
                    part = part - (4.0 * rate * rate) * (total * rest)
                outer = plus(outer, weight * part)
        return inner + (rate**4) * outer

    def load_block(layer, block, half):
        def load(ref, middle, cell):
            dz, dx, dy = cell
            row = 8 + 8 * block + dx
            return ref[dy + middle, layer - BASE + dz, half, row : row + 8, :]

        return load

    def own_block(layer, block, half):
        pair = lax.div(layer, 2) - 4
        return [triples[slot, pair, half, 8 * block : 8 * block + 8, :] for slot in range(3)]

    def halves(low, high, body):
        def step(index, carry):
            layer = low + 2 * lax.div(index, 2)
            for k in range(2):
                body(layer + k, lax.rem(index, 2), 1 if (low + k) % 2 else -1)
            return carry

        lax.fori_loop(0, high - low, step, 0)

    def plain(block):
        row = MID - 8 + 8 * block

        def body(layer, half, out):
            k2[layer, half, row : row + 8, :] = second_sums(
                load_block(layer, block, half),
                own_block(layer, block, half),
                c1[layer, half, row : row + 8, :],
                s2[layer, half, row : row + 8, :],
                out,
            )

        return body

    def merged(layer, half, out):
        high = load_block(layer, 2, half)
        low = load_block(layer, 0, half)

        def load(ref, middle, cell):
            return jnp.where(upper, high(ref, middle, cell), low(ref, middle, cell))

        def field(ref):
            return jnp.where(
                upper, ref[layer, half, MID + 8 : MID + 16, :], ref[layer, half, MID - 8 : MID, :]
            )

        own_labels = [
            jnp.where(upper, one, two)
            for one, two in zip(own_block(layer, 2, half), own_block(layer, 0, half))
        ]
        value = second_sums(load, own_labels, field(c1), field(s2), out)
        k2[layer, half, MID + 8 : MID + 16, :] = value
        k2[layer, half, MID - 8 : MID, :] = value

    halves(TILE - 7, TILE + 9, plain(1))
    halves(TILE - 2, TILE + 4, plain(0))
    halves(TILE - 2, TILE + 4, plain(2))
    halves(TILE - 6, TILE - 2, merged)
    halves(TILE + 4, TILE + 8, merged)

    for sub_step in range(1, NSUB + 1):
        source = (cx, c1)[sub_step % 2]
        target = (c1, cx)[sub_step % 2]
        put_mu, put_c = passes(k2, source, target)
        over(*near_tile(9 - 2 * sub_step), (MID,), put_mu)
        over(*near_tile(8 - 2 * sub_step), sides, put_mu)
        if sub_step < NSUB:
            over(*near_tile(8 - 2 * sub_step), (MID,), put_c)
            over(*near_tile(7 - 2 * sub_step), sides, put_c)
        else:
            for layer in (0, 1):
                for half, value in enumerate(c_at(source, TILE + layer, MID)):
                    out_ref[layer, :, half * HALF : (half + 1) * HALF] = value
    outgoing.wait()


def sintering(where, labels, dens, near_labels, near_dens, far_labels, far_dens):
    field = pltpu.VMEM((DEEP, 2, ROWS, HALF), jnp.float32)
    vmem = pl.BlockSpec(memory_space=pltpu.VMEM)
    anywhere = pl.BlockSpec(memory_space=pl.ANY)
    return pl.pallas_call(
        kernel,
        out_shape=(
            jax.ShapeDtypeStruct((GDEV, LAYERS, 8, WIDTH), jnp.float32),
            jax.ShapeDtypeStruct((2, 8, WIDTH), jnp.float32),
        ),
        in_specs=[pl.BlockSpec(memory_space=pltpu.SMEM)] + [vmem] * 5 + [anywhere],
        out_specs=(anywhere, vmem),
        scratch_shapes=[field] * 8
        + [
            pltpu.VMEM((5, 20, 2, 40, HALF), jnp.float32),
            pltpu.VMEM((5, 20, 2, 40, HALF), jnp.float32),
            pltpu.VMEM((3, 20, 2, 40, HALF), jnp.float32),
            pltpu.VMEM((DEEP, 2, 8 * GDEV, HALF), jnp.float32),
            pltpu.VMEM((DEEP, 2, 8 * GDEV, HALF), jnp.float32),
            pltpu.VMEM((GDEV, LAYERS, 8, WIDTH), jnp.float32),
            pltpu.VMEM((2, LAYERS, 8, WIDTH), jnp.float32),
            pltpu.VMEM((3, 9, 2, 24, HALF), jnp.float32),
            pltpu.SemaphoreType.DMA((2,)),
        ],
        compiler_params=pltpu.CompilerParams(vmem_limit_bytes=38 * 1024 * 1024),
        name="sintering",
    )(where, labels, dens, near_labels, near_dens, far_labels, far_dens)


def from_sides(block, distance):
    grains = lax.axis_size("grain")
    count = lax.axis_size("space")
    pairs = []
    for g in range(grains):
        way = distance if g % 2 == 0 else -distance
        for s in range(count):
            pairs.append((g * count + (s + way) % count, g * count + s))
    return lax.ppermute(block, ("grain", "space"), pairs)


def swap_cores(block):
    return lax.ppermute(block, "grain", [(i, i ^ 1) for i in range(lax.axis_size("grain"))])


def per_device(labels, density):
    grain = lax.axis_index("grain")
    named = labels.astype(jnp.float32)
    own = jnp.broadcast_to(density[None], (lax.axis_size("grain"),) + density.shape)
    dens = lax.all_to_all(own, "grain", 0, 0).reshape(LAYERS, 8, WIDTH)
    far_side, near_side = [from_sides(named, distance) for distance in (2, 1)]
    near_labels = jnp.stack([near_side, far_side])
    far_side, near_side = [from_sides(dens, distance) for distance in (2, 1)]
    near_dens = jnp.stack([near_side, far_side])
    far_labels = swap_cores(near_labels)
    far_dens = swap_cores(near_dens)
    return sintering(
        grain.reshape(1).astype(jnp.int32),
        labels,
        dens,
        near_labels,
        near_dens,
        far_labels,
        far_dens,
    )


def solution(mesh):
    return jax.shard_map(
        per_device,
        mesh=mesh,
        in_specs=(P(None, "space", None), P("grain", "space", None)),
        out_specs=(P("grain", None, "space", None), P("grain", "space", None)),
        check_vma=False,
    )
```
